256 devices in a mesh: dp: 16 (over z, x_lo), mp: 16 (over x_hi, y, core).
Axes of the slice: x: 4 (x_hi: 2, x_lo: 2; x = x_hi * 2 + x_lo), y: 4, z: 8, core: 2. Of those that a mesh axis runs over, the one named last changes fastest.
Arguments:
- grads: bfloat16 [1024, 1048576], P('dp', 'mp'), as said below
- sign_bits: int32 [1048576], P('mp'), may hold values from 0 to 1
- columns: int32 [8192], replicated, may hold values from 0 to 1048575
Outputs:
- gram: float32 [1024, 1024], P('dp', 'mp')
The draws below stay inside these ranges and needn't reach their ends.
Inputs may be any that keep to these rules, and one draw needn't show every extreme that they name: `grads`: gradients of different examples share a common direction with example-dependent coefficients, plus independent parts.
All inputs are finite; a program needn't handle non-finite values.
Results may differ from the reference program's by a relative error of at most 0.00041.
Values may be sent and summed in bfloat16 or wider, within the bound.
A program may use at most 128 MiB of HBM per device.

```python
import jax
import jax.numpy as jnp
from jax import lax

PARAMS = 1048576
SKETCH = 8192
EXAMPLES = 1024
N_MP = 16


def draw_grads(key, part):
    key = jax.random.fold_in(key, 7)
    key_noise, key_common, key_coef, key_scale = jax.random.split(key, 4)
    common = jax.random.normal(key_common, (1, PARAMS), jnp.float32)
    coef = jax.random.uniform(key_coef, (EXAMPLES, 1), jnp.float32, -1.0, 1.0)
    scales = jnp.exp(jax.random.uniform(key_scale, (EXAMPLES, 1), jnp.float32, -1.15, 1.15))
    noise = jax.random.normal(key_noise, (EXAMPLES, PARAMS), jnp.float32)
    strength = 0.7
    values = scales * (strength * coef * common + noise) / 1024.0
    return values.astype(jnp.bfloat16)


def place_ends(result, own_key, least, high):
    longest = result.shape.index(max(result.shape))
    spots = []
    for shift in (0, 1):
        where = [jax.random.randint(jax.random.fold_in(own_key, axis), (), 0, length) for axis, length in enumerate(result.shape)]
        where[longest] = (where[longest] + shift) % result.shape[longest]
        spots.append(tuple(where))
    return result.at[spots[0]].set(least).at[spots[1]].set(high)


def setup_inputs(seed: int = 0) -> dict:
    streams_of = jax.random.split(jax.random.key(seed), 4)
    return {
        "grads": draw_grads(jax.random.fold_in(streams_of[3], 71), 0),
        "sign_bits": place_ends(jax.random.randint(streams_of[1], (PARAMS,), 0, 2), jax.random.fold_in(streams_of[1], 1), 0, 1).astype(jnp.int32),
        "columns": place_ends(jax.random.randint(streams_of[2], (SKETCH,), 0, PARAMS), jax.random.fold_in(streams_of[2], 1), 0, PARAMS - 1).astype(jnp.int32),
    }


def parity_of(values, bit_count):
    parity_sum = jnp.zeros_like(values)
    for bit_place in range(bit_count):
        parity_sum = parity_sum + jnp.bitwise_and(jnp.right_shift(values, bit_place), 1)
    return parity_sum % 2

def hadamard(order):
    rows = lax.iota(jnp.int32, order)
    parity = parity_of(jnp.bitwise_and(rows[:, None], rows[None, :]), max(order - 1, 1).bit_length())
    return (1 - 2 * parity).astype(jnp.float32)

def reference(grads, sign_bits, columns):
    block_len = PARAMS // N_MP
    level = (block_len.bit_length() - 1) // 2
    size_a = 2 ** level
    size_b = block_len // size_a
    had_a = hadamard(size_a)
    had_b = hadamard(size_b)
    had_m = hadamard(N_MP)
    signs = (2 * sign_bits - 1).astype(jnp.bfloat16)
    high = (columns // block_len).astype(jnp.int32)
    low = (columns % block_len).astype(jnp.int32)
    weights = had_m[:, high]
    scale = 1.0 / jnp.sqrt(jnp.float32(SKETCH))

    def sketch_group(rows):
        signed = rows * signs[None, :]
        blocks = signed.reshape(rows.shape[0], N_MP, size_a, size_b).astype(jnp.float32)
        first = jnp.einsum('rmab,bc->rmac', blocks, had_b).astype(jnp.bfloat16)
        second = jnp.einsum('rmac,ad->rmdc', first.astype(jnp.float32), had_a)
        flat = second.reshape(rows.shape[0], N_MP, block_len)
        picked = flat[:, :, low]
        total = jnp.einsum('rmk,mk->rk', picked, weights) * scale
        return total.astype(jnp.bfloat16)
    groups = grads.reshape(EXAMPLES // 16, 16, PARAMS)
    sketch = lax.map(sketch_group, groups).reshape(EXAMPLES, SKETCH)
    return jnp.dot(sketch, sketch.T, preferred_element_type=jnp.float32)
```

```python
import functools

import jax
import jax.numpy as jnp
from jax import lax
from jax.experimental import pallas as pl
from jax.experimental.pallas import tpu as pltpu
from jax.sharding import PartitionSpec as P

SKETCH = 8192
ROWS = 64
LOCAL = 65536
CHUNKS = 16
STRIDE = 264


def parity(v, bits):
    p = v & 1
    for i in range(1, bits):
        p = p ^ ((v >> i) & 1)
    return p


def iota(shape, axis):
    return lax.broadcasted_iota(jnp.int32, shape, axis)


def hadamard(order, bits):
    both = iota((order, order), 0) & iota((order, order), 1)
    return (1 - 2 * parity(both, bits)).astype(jnp.float32).astype(jnp.bfloat16)


def local_kernel(
    grads, bits, columns, out, data, sign, cols, rows_v, rows_s, first, second, picked, sa, sb, had_b, had_a, gsem, ssem
):
    copy_sign = pltpu.make_async_copy(bits, sign, ssem.at[0])
    copy_cols = pltpu.make_async_copy(columns, cols, ssem.at[1])
    copy_cols.start()
    copy_sign.start()
    width = LOCAL // CHUNKS

    def chunk(i):
        return pltpu.make_async_copy(grads.at[:, pl.ds(i * width, width)], data.at[i], gsem.at[i])

    for i in range(CHUNKS):
        chunk(i).start()
    had_b[...] = hadamard(256, 8)
    had_a[...] = hadamard(128, 7)
    copy_cols.wait()
    cv = cols[...]
    rows_v[...] = ((cv & 255) << 7) | ((cv & 65535) >> 9)
    copy_rows = pltpu.make_async_copy(rows_v, rows_s, ssem.at[2])
    copy_rows.start()
    me = lax.axis_index("mp")
    eye = iota((128, 128), 0) == iota((128, 128), 1)
    halves = ((iota((256, 128), 0) >> 7) == (iota((256, 128), 1) >> 6)).astype(jnp.float32).astype(jnp.bfloat16)
    w = 1.0 - 2.0 * parity((cv >> 16) & me, 4).astype(jnp.float32)
    ws = w * (1.0 - 2.0 * ((cv >> 8) & 1).astype(jnp.float32))

    def spread(v1, v2):
        d = jnp.concatenate([jnp.where(eye, v1, 0.0), jnp.where(eye, v2, 0.0)], axis=1)
        return jnp.dot(d.astype(jnp.bfloat16), halves, preferred_element_type=jnp.float32)

    for j in range(16):
        for t in range(2):
            p, q = 4 * j + t, 4 * j + 2 + t
            sa[pl.ds(j * 256 + t * 128, 128), :] = spread(w[p : p + 1], ws[q : q + 1])
            sb[pl.ds(j * 256 + t * 128, 128), :] = spread(ws[p : p + 1], w[q : q + 1])
    copy_sign.wait()

    @pl.loop(0, CHUNKS)
    def _(i):
        chunk(i).wait()
        for q in range(4):
            s = (2 * sign[pl.ds(pl.multiple_of(i * 32 + q * 8, 8), 8), :] - 1).astype(jnp.float32).astype(jnp.bfloat16)
            parts = []
            for a in range(4):
                both = []
                for h in range(2):
                    x = data[i, :, pl.ds((q * 4 + a) * 256 + h * 128, 128)]
                    both.append(x * s[2 * a + h : 2 * a + h + 1, :])
                parts.append(jnp.concatenate(both, axis=1))
            block = jnp.concatenate(parts, axis=0)
            o = lax.dot_general(had_b[...], block, (((1,), (1,)), ((), ())), preferred_element_type=jnp.float32)
            g = pl.multiple_of((i * 4 + q) * (2 * STRIDE), 8)
            first[pl.ds(g, 256), :] = o[:, :128]
            first[pl.ds(pl.multiple_of(g + STRIDE, 8), 256), :] = o[:, 128:]

    @pl.loop(0, 32)
    def _(i):
        for q in range(4):
            c = i * 8 + q * 2
            z0 = first[pl.ds(c, 128, stride=STRIDE), :].astype(jnp.bfloat16)
            z1 = first[pl.ds(c + 1, 128, stride=STRIDE), :].astype(jnp.bfloat16)
            o = jnp.dot(had_a[...], jnp.concatenate([z0, z1], axis=1), preferred_element_type=jnp.float32)
            second[pl.ds(pl.multiple_of(c * 128, 128), 128), :] = o[:, :128]
            second[pl.ds(pl.multiple_of(c * 128 + 128, 128), 128), :] = o[:, 128:]

    copy_rows.wait()

    @pl.loop(0, 16)
    def _(j):
        @pl.loop(0, 2)
        def _(u):
            for h in range(2):
                for b in range(8):
                    at = [rows_s[j * 4 + u + 2 * h, b * 16 + e] for e in range(16)]
                    got = [second[pl.ds(r, 1), :] for r in at]
                    for e in range(16):
                        picked[h, pl.ds(u * 128 + b * 16 + e, 1), :] = got[e]

        low = iota((256, 128), 1) < 64
        x = picked[0]
        y = picked[1]
        here = pl.ds(pl.multiple_of(j * 256, 256), 256)
        out[here, :] = (
            jnp.where(low, x, y) * sa[here, :] + pltpu.roll(jnp.where(low, y, x), 64, 1) * sb[here, :]
        )


def local(grads, sign_bits, columns):
    return pl.pallas_call(
        local_kernel,
        out_shape=jax.ShapeDtypeStruct((4096, 128), jnp.float32),
        in_specs=[pl.BlockSpec(memory_space=pl.ANY)] * 3,
        out_specs=pl.BlockSpec(memory_space=pltpu.VMEM),
        scratch_shapes=[
            pltpu.VMEM((CHUNKS, ROWS, LOCAL // CHUNKS), jnp.bfloat16),
            pltpu.VMEM((512, 128), jnp.int32),
            pltpu.VMEM((64, 128), jnp.int32),
            pltpu.VMEM((64, 128), jnp.int32),
            pltpu.SMEM((64, 128), jnp.int32),
            pltpu.VMEM((128 * STRIDE, 128), jnp.float32),
            pltpu.VMEM((32768, 128), jnp.float32),
            pltpu.VMEM((2, 256, 128), jnp.float32),
            pltpu.VMEM((4096, 128), jnp.float32),
            pltpu.VMEM((4096, 128), jnp.float32),
            pltpu.VMEM((256, 256), jnp.bfloat16),
            pltpu.VMEM((128, 128), jnp.bfloat16),
            pltpu.SemaphoreType.DMA((CHUNKS,)),
            pltpu.SemaphoreType.DMA((3,)),
        ],
        compiler_params=pltpu.CompilerParams(vmem_limit_bytes=60 * 2**20),
    )(grads, sign_bits.reshape(512, 128), columns.reshape(64, 128))


def per_device(grads, sign_bits, columns):
    terms = local(grads, sign_bits, columns)
    scale = 1.0 / jnp.sqrt(jnp.float32(SKETCH))
    sketch = (lax.psum_scatter(terms, "mp", scatter_dimension=0, tiled=True) * scale).astype(jnp.bfloat16)
    everyone = lax.all_gather(sketch, "dp", axis=0, tiled=False)
    partial_gram = jnp.einsum(
        "khn,zkhe->nze",
        sketch.reshape(256, 2, ROWS),
        everyone.reshape(16, 256, 2, ROWS),
        preferred_element_type=jnp.float32,
    ).reshape(ROWS, 16 * ROWS)
    return lax.psum_scatter(partial_gram, "mp", scatter_dimension=1, tiled=True)


def solution(mesh):
    return jax.shard_map(
        per_device,
        mesh=mesh,
        in_specs=(P("dp", "mp"), P("mp"), P()),
        out_specs=P("dp", "mp"),
        check_vma=False,
    )
```

```python
import functools

import jax
import jax.numpy as jnp
from jax import lax
from jax.experimental import pallas as pl
from jax.experimental.pallas import tpu as pltpu
from jax.sharding import PartitionSpec as P

SKETCH = 8192
ROWS = 64
LOCAL = 65536
CHUNKS = 16
STRIDE = 264
MESH = pl.DeviceIdType.MESH
SCALE = 1.0 / SKETCH**0.5


def parity(v, bits):
    p = v & 1
    for i in range(1, bits):
        p = p ^ ((v >> i) & 1)
    return p


def iota(shape, axis):
    return lax.broadcasted_iota(jnp.int32, shape, axis)


def hadamard(order, bits):
    both = iota((order, order), 0) & iota((order, order), 1)
    return (1 - 2 * parity(both, bits)).astype(jnp.float32).astype(jnp.bfloat16)


def kernel(
    grads, bits, columns, out,
    data, sign, cols, rows_v, rows_s, first, second, picked, sa, sb, had_b, had_a,
    pair_out, pair_in, own, sum_out, sum_in, ring, beside, left_t, block_out, block_in,
    gsem, ssem, pair_send, pair_recv, sum_send, sum_recv, right_send, left_send, ring_recv, x_send, x_recv, block_send, block_recv,
):
    me = lax.axis_index("mp")
    dp = lax.axis_index("dp")
    core, chip = lax.rem(me, 2), me // 2
    x, z = lax.rem(dp, 2), dp // 2
    right, left = lax.rem(z + 1, 8), lax.rem(z + 7, 8)
    alone = x == core

    barrier = pltpu.get_barrier_semaphore()

    def greet(d, m):
        pl.semaphore_signal(barrier, inc=1, device_id=(d, m), device_id_type=MESH)

    greet(dp, 2 * chip + 1 - core)
    for o in range(1, 8):
        greet(dp, 2 * lax.rem(chip + o, 8) + core)
    greet(2 * z + 1 - x, me)
    greet(2 * left + x, me)
    greet(2 * right + x, me)

    @pl.loop(0, 16)
    def _(q):
        @pl.when(jnp.logical_not(jnp.logical_and(alone, q == me)))
        def _():
            greet(2 * z + core, q)

    copy_sign = pltpu.make_async_copy(bits, sign, ssem.at[0])
    copy_cols = pltpu.make_async_copy(columns, cols, ssem.at[1])
    copy_cols.start()
    copy_sign.start()
    width = LOCAL // CHUNKS

    def chunk(i):
        return pltpu.make_async_copy(grads.at[:, pl.ds(i * width, width)], data.at[i], gsem.at[i])

    for i in range(CHUNKS):
        chunk(i).start()
    had_b[...] = hadamard(256, 8)
    had_a[...] = hadamard(128, 7)
    copy_cols.wait()
    cv = cols[...]
    rows_v[...] = ((cv & 255) << 7) | ((cv & 65535) >> 9)
    copy_rows = pltpu.make_async_copy(rows_v, rows_s, ssem.at[2])
    copy_rows.start()
    eye = iota((128, 128), 0) == iota((128, 128), 1)
    halves = ((iota((256, 128), 0) >> 7) == (iota((256, 128), 1) >> 6)).astype(jnp.float32).astype(jnp.bfloat16)
    w = 1.0 - 2.0 * parity((cv >> 16) & me, 4).astype(jnp.float32)
    ws = w * (1.0 - 2.0 * ((cv >> 8) & 1).astype(jnp.float32))

    def spread(v1, v2):
        d = jnp.concatenate([jnp.where(eye, v1, 0.0), jnp.where(eye, v2, 0.0)], axis=1)
        return jnp.dot(d.astype(jnp.bfloat16), halves, preferred_element_type=jnp.float32)

    for j in range(16):
        for t in range(2):
            p, q = 4 * j + t, 4 * j + 2 + t
            sa[pl.ds(j * 256 + t * 128, 128), :] = spread(w[p : p + 1], ws[q : q + 1])
            sb[pl.ds(j * 256 + t * 128, 128), :] = spread(ws[p : p + 1], w[q : q + 1])
    copy_sign.wait()

    @pl.loop(0, CHUNKS)
    def _(i):
        chunk(i).wait()
        for q in range(4):
            s = (2 * sign[pl.ds(pl.multiple_of(i * 32 + q * 8, 8), 8), :] - 1).astype(jnp.float32).astype(jnp.bfloat16)
            parts = []
            for a in range(4):
                both = []
                for h in range(2):
                    v = data[i, :, pl.ds((q * 4 + a) * 256 + h * 128, 128)]
                    both.append(v * s[2 * a + h : 2 * a + h + 1, :])
                parts.append(jnp.concatenate(both, axis=1))
            block = jnp.concatenate(parts, axis=0)
            o = lax.dot_general(had_b[...], block, (((1,), (1,)), ((), ())), preferred_element_type=jnp.float32)
            g = pl.multiple_of((i * 4 + q) * (2 * STRIDE), 8)
            first[pl.ds(g, 256), :] = o[:, :128]
            first[pl.ds(pl.multiple_of(g + STRIDE, 8), 256), :] = o[:, 128:]

    @pl.loop(0, 32)
    def _(i):
        for q in range(4):
            c = i * 8 + q * 2
            z0 = first[pl.ds(c, 128, stride=STRIDE), :].astype(jnp.bfloat16)
            z1 = first[pl.ds(c + 1, 128, stride=STRIDE), :].astype(jnp.bfloat16)
            o = jnp.dot(had_a[...], jnp.concatenate([z0, z1], axis=1), preferred_element_type=jnp.float32)
            second[pl.ds(pl.multiple_of(c * 128, 128), 128), :] = o[:, :128]
            second[pl.ds(pl.multiple_of(c * 128 + 128, 128), 128), :] = o[:, 128:]

    copy_rows.wait()

    def gather(j, dst, at_chip):
        @pl.loop(0, 2)
        def _(u):
            for h in range(2):
                for b in range(8):
                    at = [rows_s[j * 4 + u + 2 * h, b * 16 + e] for e in range(16)]
                    got = [second[pl.ds(r, 1), :] for r in at]
                    for e in range(16):
                        picked[h, pl.ds(u * 128 + b * 16 + e, 1), :] = got[e]

        low = iota((256, 128), 1) < 64
        p = picked[0]
        q = picked[1]
        here = pl.ds(pl.multiple_of(j * 256, 256), 256)
        dst[at_chip] = (
            jnp.where(low, p, q) * sa[here, :] + pltpu.roll(jnp.where(low, q, p), 64, 1) * sb[here, :]
        )

    def to_pair(t):
        return pltpu.make_async_remote_copy(
            pair_out.at[t], pair_in.at[t], pair_send.at[t], pair_recv.at[t],
            device_id=(dp, 2 * chip + 1 - core), device_id_type=MESH,
        )

    def to_chip(t, slot):
        return pltpu.make_async_remote_copy(
            sum_out.at[t], sum_in.at[slot], sum_send.at[t], sum_recv.at[slot],
            device_id=(dp, 2 * t + core), device_id_type=MESH,
        )

    @pl.when(alone)
    def _():
        pl.semaphore_wait(barrier, 26)

    @pl.when(jnp.logical_not(alone))
    def _():
        pl.semaphore_wait(barrier, 27)

    @pl.loop(0, 9)
    def _(s):
        @pl.when(s < 8)
        def _():
            t = lax.rem(chip + 1 + s, 8)
            gather(2 * t + 1 - core, pair_out, t)
            to_pair(t).start()
            gather(2 * t + core, own, t)

        @pl.when(s > 0)
        def _():
            t = lax.rem(chip + s, 8)
            to_pair(t).wait_recv()

            @pl.when(s < 8)
            def _():
                sum_out[t] = (own[t] + pair_in[t]).astype(jnp.bfloat16)
                to_chip(t, chip).start()

    total = own[chip] + pair_in[chip]
    for o in range(1, 8):
        t = lax.rem(chip + o, 8)
        to_chip(t, t).wait_recv()
        total += sum_in[t].astype(jnp.float32)
    ring[z] = (total * SCALE).astype(jnp.bfloat16)

    def to_right(k):
        slot = lax.rem(z + 8 - k, 8)
        return pltpu.make_async_remote_copy(
            ring.at[slot], ring.at[slot], right_send.at[k], ring_recv.at[slot],
            device_id=(2 * right + x, me), device_id_type=MESH,
        )

    def to_left(k):
        slot = lax.rem(z + k, 8)
        return pltpu.make_async_remote_copy(
            ring.at[slot], ring.at[slot], left_send.at[k], ring_recv.at[slot],
            device_id=(2 * left + x, me), device_id_type=MESH,
        )

    def arrived(slot):
        pltpu.make_async_remote_copy(
            ring.at[slot], ring.at[slot], right_send.at[0], ring_recv.at[slot],
            device_id=(2 * right + x, me), device_id_type=MESH,
        ).wait_recv()

    to_x = pltpu.make_async_remote_copy(
        ring.at[z], beside, x_send, x_recv, device_id=(2 * z + 1 - x, me), device_id_type=MESH
    )
    to_x.start()
    to_right(0).start()
    to_left(0).start()

    def to_owner(k, d, m, slot):
        return pltpu.make_async_remote_copy(
            block_out.at[k], block_in.at[slot], block_send.at[k], block_recv.at[slot],
            device_id=(d, m), device_id_type=MESH,
        )

    def products(slot):
        p = jnp.dot(left_t[...], ring[slot], preferred_element_type=jnp.float32)
        low = iota((32, 128), 1) < 64
        for rel in range(2):
            lo, hi = p[rel * 128 : rel * 128 + 64], p[rel * 128 + 64 : rel * 128 + 128]
            a0, b0, a1, b1 = lo[:32], lo[32:], hi[:32], hi[32:]
            both = jnp.where(low, a0, b1) + pltpu.roll(jnp.where(low, b0, a1), 64, 1)
            if rel == 0:
                mine = jnp.logical_and(alone, slot == chip)

                @pl.when(mine)
                def _():
                    block_in[me] = both

                @pl.when(jnp.logical_not(mine))
                def _():
                    block_out[2 * slot] = both
                    to_owner(2 * slot, dp, 2 * slot + x, me).start()

            else:
                block_out[2 * slot + 1] = both
                to_owner(2 * slot + 1, 2 * z + 1 - x, 2 * slot + x, me).start()

    left_t[pl.ds(0, 128), :] = ring[z].astype(jnp.float32).T.astype(jnp.bfloat16)
    to_x.wait_recv()
    left_t[pl.ds(128, 128), :] = beside[...].astype(jnp.float32).T.astype(jnp.bfloat16)
    products(z)
    for k in range(1, 5):
        down, up = lax.rem(z + 8 - k, 8), lax.rem(z + k, 8)
        arrived(down)
        if k < 4:
            to_right(k).start()
            arrived(up)
        if k < 3:
            to_left(k).start()
        products(down)
        if k < 4:
            products(up)

    @pl.loop(0, 16)
    def _(q):
        @pl.when(jnp.logical_not(jnp.logical_and(alone, q == me)))
        def _():
            to_owner(0, dp, me, q).wait_recv()

    result = block_in[0]
    for q in range(1, 16):
        result += block_in[q]
    out[pl.ds(0, 32), :] = result[:, :64]
    out[pl.ds(32, 32), :] = result[:, 64:]

    for t in range(8):
        to_pair(t).wait_send()
    for o in range(1, 8):
        to_chip(lax.rem(chip + o, 8), chip).wait_send()
    to_x.wait_send()
    for k in range(4):
        to_right(k).wait_send()
    for k in range(3):
        to_left(k).wait_send()

    @pl.loop(0, 8)
    def _(slot):
        to_owner(2 * slot + 1, dp, me, me).wait_send()

        @pl.when(jnp.logical_not(jnp.logical_and(alone, slot == chip)))
        def _():
            to_owner(2 * slot, dp, me, me).wait_send()


def per_device(grads, sign_bits, columns):
    f32, bf16 = jnp.float32, jnp.bfloat16
    dma = pltpu.SemaphoreType.DMA
    return pl.pallas_call(
        kernel,
        out_shape=jax.ShapeDtypeStruct((ROWS, ROWS), f32),
        in_specs=[pl.BlockSpec(memory_space=pl.ANY)] * 3,
        out_specs=pl.BlockSpec(memory_space=pltpu.VMEM),
        scratch_shapes=[
            pltpu.VMEM((CHUNKS, ROWS, LOCAL // CHUNKS), bf16),
            pltpu.VMEM((512, 128), jnp.int32),
            pltpu.VMEM((64, 128), jnp.int32),
            pltpu.VMEM((64, 128), jnp.int32),
            pltpu.SMEM((64, 128), jnp.int32),
            pltpu.VMEM((128 * STRIDE, 128), f32),
            pltpu.VMEM((32768, 128), f32),
            pltpu.VMEM((2, 256, 128), f32),
            pltpu.VMEM((4096, 128), f32),
            pltpu.VMEM((4096, 128), f32),
            pltpu.VMEM((256, 256), bf16),
            pltpu.VMEM((128, 128), bf16),
            pltpu.VMEM((8, 256, 128), f32),
            pltpu.VMEM((8, 256, 128), f32),
            pltpu.VMEM((8, 256, 128), f32),
            pltpu.VMEM((8, 256, 128), bf16),
            pltpu.VMEM((8, 256, 128), bf16),
            pltpu.VMEM((8, 256, 128), bf16),
            pltpu.VMEM((256, 128), bf16),
            pltpu.VMEM((256, 256), bf16),
            pltpu.VMEM((16, 32, 128), f32),
            pltpu.VMEM((16, 32, 128), f32),
            dma((CHUNKS,)),
            dma((3,)),
            dma((8,)),
            dma((8,)),
            dma((8,)),
            dma((8,)),
            dma((4,)),
            dma((3,)),
            dma((8,)),
            dma,
            dma,
            dma((16,)),
            dma((16,)),
        ],
        compiler_params=pltpu.CompilerParams(
            vmem_limit_bytes=60 * 2**20, collective_id=0, has_side_effects=True
        ),
    )(grads, sign_bits.reshape(512, 128), columns.reshape(64, 128))


def solution(mesh):
    return jax.shard_map(
        per_device,
        mesh=mesh,
        in_specs=(P("dp", "mp"), P("mp"), P()),
        out_specs=P("dp", "mp"),
        check_vma=False,
    )
```

```python
import functools

import jax
import jax.numpy as jnp
from jax import lax
from jax.experimental import pallas as pl
from jax.experimental.pallas import tpu as pltpu
from jax.sharding import PartitionSpec as P

SKETCH = 8192
ROWS = 64
LOCAL = 65536
CHUNKS = 2
STRIDE = 265
MESH = pl.DeviceIdType.MESH
SCALE = 1.0 / SKETCH**0.5


def parity(v, bits):
    p = v & 1
    for i in range(1, bits):
        p = p ^ ((v >> i) & 1)
    return p


def iota(shape, axis):
    return lax.broadcasted_iota(jnp.int32, shape, axis)


def hadamard(order, bits):
    both = iota((order, order), 0) & iota((order, order), 1)
    return (1 - 2 * parity(both, bits)).astype(jnp.float32).astype(jnp.bfloat16)


def kernel(
    grads, bits, columns, out,
    data, sign, cols, rows_v, rows_s, first, second, picked, sa, sb, had_b, had_a,
    pair_out, pair_in, own, sum_out, sum_in, ring, beside, left_t, block_out, block_in,
    gsem, ssem, pair_send, pair_recv, sum_send, sum_recv, ring_send, ring_recv, half_recv, x_send, x_recv, block_send, block_recv,
):
    me = lax.axis_index("mp")
    dp = lax.axis_index("dp")
    core, chip = lax.rem(me, 2), me // 2
    x, z = lax.rem(dp, 2), dp // 2
    alone = x == core

    copy_sign = pltpu.make_async_copy(bits, sign, ssem.at[0])
    copy_cols = pltpu.make_async_copy(columns, cols, ssem.at[1])
    copy_cols.start()
    copy_sign.start()
    width = LOCAL // CHUNKS

    def chunk(i):
        return pltpu.make_async_copy(grads.at[:, pl.ds(i * width, width)], data.at[i], gsem.at[i])

    for i in range(CHUNKS):
        chunk(i).start()
    barrier = pltpu.get_barrier_semaphore()

    def greet(d, m):
        pl.semaphore_signal(barrier, inc=1, device_id=(d, m), device_id_type=MESH)

    greet(dp, 2 * chip + 1 - core)
    for o in range(1, 8):
        greet(dp, 2 * lax.rem(chip + o, 8) + core)
    greet(2 * z + 1 - x, me)
    for o in (1, 2, 6, 7):
        greet(2 * lax.rem(z + o, 8) + x, me)

    @pl.loop(0, 16)
    def _(q):
        @pl.when(jnp.logical_not(jnp.logical_and(alone, q == me)))
        def _():
            greet(2 * z + core, q)

    had_b[...] = hadamard(256, 8)
    had_a[...] = hadamard(128, 7)
    copy_cols.wait()
    cv = cols[...]
    at_rows = (((cv & 255) << 7) | ((cv & 65535) >> 9)).reshape(8, 8, 128)
    rows_v[...] = jnp.where(core == 1, at_rows, pltpu.roll(at_rows, 4, 1))

    def window(s, w):
        return pltpu.make_async_copy(rows_v.at[lax.rem(chip + 1 + s, 8)], rows_s.at[w], ssem.at[2 + w])

    window(0, 0).start()
    window(1, 1).start()
    eye = iota((128, 128), 0) == iota((128, 128), 1)
    halves = ((iota((256, 128), 0) >> 7) == (iota((256, 128), 1) >> 6)).astype(jnp.float32).astype(jnp.bfloat16)
    w = 1.0 - 2.0 * parity((cv >> 16) & me, 4).astype(jnp.float32)
    ws = w * (1.0 - 2.0 * ((cv >> 8) & 1).astype(jnp.float32))

    def spread(v1, v2):
        d = jnp.concatenate([jnp.where(eye, v1, 0.0), jnp.where(eye, v2, 0.0)], axis=1)
        return jnp.dot(d.astype(jnp.bfloat16), halves, preferred_element_type=jnp.float32)

    for j in range(16):
        for t in range(2):
            p, q = 4 * j + t, 4 * j + 2 + t
            sa[pl.ds(j * 256 + t * 128, 128), :] = spread(w[p : p + 1], ws[q : q + 1])
            sb[pl.ds(j * 256 + t * 128, 128), :] = spread(ws[p : p + 1], w[q : q + 1])
    copy_sign.wait()

    @pl.loop(0, CHUNKS)
    def _(i):
        chunk(i).wait()
        for q in range(64 // CHUNKS):
            s = (2 * sign[pl.ds(pl.multiple_of(i * (512 // CHUNKS) + q * 8, 8), 8), :] - 1).astype(jnp.float32).astype(jnp.bfloat16)
            parts = []
            for a in range(4):
                both = []
                for h in range(2):
                    v = data[i, :, pl.ds((q * 4 + a) * 256 + h * 128, 128)]
                    both.append(v * s[2 * a + h : 2 * a + h + 1, :])
                parts.append(jnp.concatenate(both, axis=1))
            block = jnp.concatenate(parts, axis=0)
            o = lax.dot_general(had_b[...], block, (((1,), (1,)), ((), ())), preferred_element_type=jnp.float32)
            g = (i * (64 // CHUNKS) + q) * (2 * STRIDE)
            first[pl.ds(g, 256), :] = o[:, :128]
            first[pl.ds(g + STRIDE, 256), :] = o[:, 128:]

    @pl.loop(0, 4)
    def _(i):
        for q in range(32):
            c = (i * 32 + q) * 2
            z0 = first[pl.ds(c, 128, stride=STRIDE), :].astype(jnp.bfloat16)
            z1 = first[pl.ds(c + 1, 128, stride=STRIDE), :].astype(jnp.bfloat16)
            o = jnp.dot(had_a[...], jnp.concatenate([z0, z1], axis=1), preferred_element_type=jnp.float32)
            second[pl.ds(pl.multiple_of(c * 128, 128), 128), :] = o[:, :128]
            second[pl.ds(pl.multiple_of(c * 128 + 128, 128), 128), :] = o[:, 128:]

    low = iota((128, 128), 1) < 64

    def gather(w, which, j, dst, at_chip):
        for u in range(2):
            for h in range(2):
                spot = (which * 2 + u) * 2 + h
                for b in range(8):
                    at = [rows_s[w, which * 4 + 2 * h + u, b * 16 + e] for e in range(16)]
                    got = [second[pl.ds(r, 1), :] for r in at]
                    for e in range(16):
                        picked[spot, pl.ds(b * 16 + e, 1), :] = got[e]
        for u in range(2):
            p = picked[(which * 2 + u) * 2]
            q = picked[(which * 2 + u) * 2 + 1]
            here = pl.ds(pl.multiple_of(j * 256 + u * 128, 128), 128)
            dst[at_chip, pl.ds(u * 128, 128), :] = (
                jnp.where(low, p, q) * sa[here, :] + pltpu.roll(jnp.where(low, q, p), 64, 1) * sb[here, :]
            )

    def to_pair(t):
        return pltpu.make_async_remote_copy(
            pair_out.at[t], pair_in.at[t], pair_send.at[t], pair_recv.at[t],
            device_id=(dp, 2 * chip + 1 - core), device_id_type=MESH,
        )

    def to_chip(t, slot):
        return pltpu.make_async_remote_copy(
            sum_out.at[t], sum_in.at[slot], sum_send.at[t], sum_recv.at[slot],
            device_id=(dp, 2 * t + core), device_id_type=MESH,
        )

    @pl.when(alone)
    def _():
        pl.semaphore_wait(barrier, 28)

    @pl.when(jnp.logical_not(alone))
    def _():
        pl.semaphore_wait(barrier, 29)

    def add_pair(t):
        to_pair(t).wait_recv()
        sum_out[t] = (own[t] + pair_in[t]).astype(jnp.bfloat16)
        to_chip(t, chip).start()

    @pl.loop(0, 4)
    def _(i):
        for w in range(2):
            s = 2 * i + w
            t = lax.rem(chip + 1 + s, 8)
            window(s, w).wait()
            gather(w, 0, 2 * t + 1 - core, pair_out, t)
            to_pair(t).start()
            gather(w, 1, 2 * t + core, own, t)

            @pl.when(i < 3)
            def _():
                window(s + 2, w).start()

            if w == 1:
                add_pair(lax.rem(chip + s, 8))
            else:

                @pl.when(i > 0)
                def _():
                    add_pair(lax.rem(chip + s, 8))

    to_pair(chip).wait_recv()
    total = own[chip] + pair_in[chip]
    for o in range(1, 8):
        t = lax.rem(chip + o, 8)
        to_chip(t, t).wait_recv()
        total += sum_in[t].astype(jnp.float32)
    ring[z] = (total * SCALE).astype(jnp.bfloat16)

    def along(n, slot, part, sem):
        here = ring.at[slot, pl.ds(0, 256)] if part is None else ring.at[slot, pl.ds(part * 128, 128)]
        got = half_recv if part == 1 else ring_recv.at[slot]
        return pltpu.make_async_remote_copy(
            here, here, ring_send.at[sem], got, device_id=(2 * lax.rem(z + n, 8) + x, me), device_id_type=MESH
        )

    def arrived(slot):
        along(1, slot, None, 0).wait_recv()

    def at(n):
        return lax.rem(z + n, 8)

    to_x = pltpu.make_async_remote_copy(
        ring.at[z], beside, x_send, x_recv, device_id=(2 * z + 1 - x, me), device_id_type=MESH
    )
    sent = [along(2, z, None, 0), along(6, z, None, 1), along(1, z, None, 2), along(7, z, None, 3)]
    to_x.start()
    for copy in sent:
        copy.start()

    def to_owner(k, d, m, slot):
        return pltpu.make_async_remote_copy(
            block_out.at[k], block_in.at[slot], block_send.at[k], block_recv.at[slot],
            device_id=(d, m), device_id_type=MESH,
        )

    def products(slot):
        p = jnp.dot(left_t[...], ring[slot], preferred_element_type=jnp.float32)
        low = iota((32, 128), 1) < 64
        for rel in range(2):
            lo, hi = p[rel * 128 : rel * 128 + 64], p[rel * 128 + 64 : rel * 128 + 128]
            a0, b0, a1, b1 = lo[:32], lo[32:], hi[:32], hi[32:]
            both = jnp.where(low, a0, b1) + pltpu.roll(jnp.where(low, b0, a1), 64, 1)
            if rel == 0:
                mine = jnp.logical_and(alone, slot == chip)

                @pl.when(mine)
                def _():
                    block_in[me] = both

                @pl.when(jnp.logical_not(mine))
                def _():
                    block_out[2 * slot] = both
                    to_owner(2 * slot, dp, 2 * slot + x, me).start()

            else:
                block_out[2 * slot + 1] = both
                to_owner(2 * slot + 1, 2 * z + 1 - x, 2 * slot + x, me).start()

    left_t[pl.ds(0, 128), :] = ring[z].astype(jnp.float32).T.astype(jnp.bfloat16)
    to_x.wait_recv()
    left_t[pl.ds(128, 128), :] = beside[...].astype(jnp.float32).T.astype(jnp.bfloat16)
    products(z)
    for n, back, part in ((6, 1, 0), (2, 7, 1)):
        arrived(at(n))
        sent += [along(back, at(n), None, 4 + 2 * part), along(8 - n, at(n), part, 5 + 2 * part)]
        sent[-2].start()
        sent[-1].start()
    for n in (7, 1):
        arrived(at(n))
        products(at(n))
    products(at(6))
    products(at(2))
    for n in (5, 3):
        arrived(at(n))
        products(at(n))
    along(2, at(4), 0, 0).wait_recv()
    along(6, at(4), 1, 0).wait_recv()
    products(at(4))

    @pl.loop(0, 16)
    def _(q):
        @pl.when(jnp.logical_not(jnp.logical_and(alone, q == me)))
        def _():
            to_owner(0, dp, me, q).wait_recv()

    result = block_in[0]
    for q in range(1, 16):
        result += block_in[q]
    out[pl.ds(0, 32), :] = result[:, :64]
    out[pl.ds(32, 32), :] = result[:, 64:]

    for t in range(8):
        to_pair(t).wait_send()
    for o in range(1, 8):
        to_chip(lax.rem(chip + o, 8), chip).wait_send()
    to_x.wait_send()
    for copy in sent:
        copy.wait_send()

    @pl.loop(0, 8)
    def _(slot):
        to_owner(2 * slot + 1, dp, me, me).wait_send()

        @pl.when(jnp.logical_not(jnp.logical_and(alone, slot == chip)))
        def _():
            to_owner(2 * slot, dp, me, me).wait_send()


def per_device(grads, sign_bits, columns):
    f32, bf16 = jnp.float32, jnp.bfloat16
    dma = pltpu.SemaphoreType.DMA
    return pl.pallas_call(
        kernel,
        out_shape=jax.ShapeDtypeStruct((ROWS, ROWS), f32),
        in_specs=[pl.BlockSpec(memory_space=pl.ANY)] * 3,
        out_specs=pl.BlockSpec(memory_space=pltpu.VMEM),
        scratch_shapes=[
            pltpu.VMEM((CHUNKS, ROWS, LOCAL // CHUNKS), bf16),
            pltpu.VMEM((512, 128), jnp.int32),
            pltpu.VMEM((64, 128), jnp.int32),
            pltpu.VMEM((8, 8, 128), jnp.int32),
            pltpu.SMEM((2, 8, 128), jnp.int32),
            pltpu.VMEM((128 * STRIDE, 128), f32),
            pltpu.VMEM((32768, 128), f32),
            pltpu.VMEM((8, 128, 128), f32),
            pltpu.VMEM((4096, 128), f32),
            pltpu.VMEM((4096, 128), f32),
            pltpu.VMEM((256, 256), bf16),
            pltpu.VMEM((128, 128), bf16),
            pltpu.VMEM((8, 256, 128), f32),
            pltpu.VMEM((8, 256, 128), f32),
            pltpu.VMEM((8, 256, 128), f32),
            pltpu.VMEM((8, 256, 128), bf16),
            pltpu.VMEM((8, 256, 128), bf16),
            pltpu.VMEM((8, 256, 128), bf16),
            pltpu.VMEM((256, 128), bf16),
            pltpu.VMEM((256, 256), bf16),
            pltpu.VMEM((16, 32, 128), f32),
            pltpu.VMEM((16, 32, 128), f32),
            dma((CHUNKS,)),
            dma((4,)),
            dma((8,)),
            dma((8,)),
            dma((8,)),
            dma((8,)),
            dma((8,)),
            dma((8,)),
            dma,
            dma,
            dma,
            dma((16,)),
            dma((16,)),
        ],
        compiler_params=pltpu.CompilerParams(
            vmem_limit_bytes=60 * 2**20, collective_id=0, has_side_effects=True
        ),
    )(grads, sign_bits.reshape(512, 128), columns.reshape(64, 128))


def solution(mesh):
    return jax.shard_map(
        per_device,
        mesh=mesh,
        in_specs=(P("dp", "mp"), P("mp"), P()),
        out_specs=P("dp", "mp"),
        check_vma=False,
    )
```

```python
import functools

import jax
import jax.numpy as jnp
from jax import lax
from jax.experimental import pallas as pl
from jax.experimental.pallas import tpu as pltpu
from jax.sharding import PartitionSpec as P

SKETCH = 8192
ROWS = 64
LOCAL = 65536
CHUNKS = 2
STRIDE = 265
MESH = pl.DeviceIdType.MESH
SCALE = 1.0 / SKETCH**0.5


def parity(v, bits):
    p = v & 1
    for i in range(1, bits):
        p = p ^ ((v >> i) & 1)
    return p


def iota(shape, axis):
    return lax.broadcasted_iota(jnp.int32, shape, axis)


def hadamard(order, bits):
    both = iota((order, order), 0) & iota((order, order), 1)
    return (1 - 2 * parity(both, bits)).astype(jnp.float32).astype(jnp.bfloat16)


def kernel(
    grads, bits, columns, out,
    data, sign, cols, rows_v, rows_s, first, second, picked, sa, sb, had_b, had_a,
    pair_out, pair_in, own, sum_out, sum_in, ring, beside, left_t, block_out, block_in,
    gsem, ssem, pair_send, pair_recv, sum_send, sum_recv, ring_send, ring_recv, x_send, x_recv, block_send, block_recv,
):
    me = lax.axis_index("mp")
    dp = lax.axis_index("dp")
    core, chip = lax.rem(me, 2), me // 2
    x, z = lax.rem(dp, 2), dp // 2
    alone = x == core

    copy_sign = pltpu.make_async_copy(bits, sign, ssem.at[0])
    copy_cols = pltpu.make_async_copy(columns, cols, ssem.at[1])
    copy_cols.start()
    copy_sign.start()
    width = LOCAL // CHUNKS

    def chunk(i):
        return pltpu.make_async_copy(grads.at[:, pl.ds(i * width, width)], data.at[i], gsem.at[i])

    for i in range(CHUNKS):
        chunk(i).start()
    barrier = pltpu.get_barrier_semaphore()

    def greet(d, m):
        pl.semaphore_signal(barrier, inc=1, device_id=(d, m), device_id_type=MESH)

    greet(dp, 2 * chip + 1 - core)
    for o in range(1, 8):
        greet(dp, 2 * lax.rem(chip + o, 8) + core)
    greet(2 * z + 1 - x, me)
    for o in (1, 2, 6, 7):
        greet(2 * lax.rem(z + o, 8) + x, me)

    @pl.loop(0, 16)
    def _(q):
        @pl.when(jnp.logical_not(jnp.logical_and(alone, q == me)))
        def _():
            greet(2 * z + core, q)

    had_b[...] = hadamard(256, 8)
    had_a[...] = hadamard(128, 7)
    copy_cols.wait()
    cv = cols[...]
    at_rows = (((cv & 255) << 7) | ((cv & 65535) >> 9)).reshape(8, 8, 128)
    rows_v[...] = jnp.where(core == 1, at_rows, pltpu.roll(at_rows, 4, 1))

    across, y = chip // 4, lax.rem(chip, 4)

    def served(i, w):
        dx = 1 - (i + 2 * w) // 3
        return 4 * lax.rem(across + dx, 2) + lax.rem(y + 2 - w + i, 4)

    def window(i, w):
        return pltpu.make_async_copy(rows_v.at[served(i, w)], rows_s.at[w], ssem.at[2 + w])

    window(0, 0).start()
    window(0, 1).start()
    eye = iota((128, 128), 0) == iota((128, 128), 1)
    halves = ((iota((256, 128), 0) >> 7) == (iota((256, 128), 1) >> 6)).astype(jnp.float32).astype(jnp.bfloat16)
    w = 1.0 - 2.0 * parity((cv >> 16) & me, 4).astype(jnp.float32)
    ws = w * (1.0 - 2.0 * ((cv >> 8) & 1).astype(jnp.float32))

    def spread(v1, v2):
        d = jnp.concatenate([jnp.where(eye, v1, 0.0), jnp.where(eye, v2, 0.0)], axis=1)
        return jnp.dot(d.astype(jnp.bfloat16), halves, preferred_element_type=jnp.float32)

    for j in range(16):
        for t in range(2):
            p, q = 4 * j + t, 4 * j + 2 + t
            sa[pl.ds(j * 256 + t * 128, 128), :] = spread(w[p : p + 1], ws[q : q + 1])
            sb[pl.ds(j * 256 + t * 128, 128), :] = spread(ws[p : p + 1], w[q : q + 1])
    copy_sign.wait()

    @pl.loop(0, CHUNKS)
    def _(i):
        chunk(i).wait()
        for q in range(64 // CHUNKS):
            s = (2 * sign[pl.ds(pl.multiple_of(i * (512 // CHUNKS) + q * 8, 8), 8), :] - 1).astype(jnp.float32).astype(jnp.bfloat16)
            parts = []
            for a in range(4):
                both = []
                for h in range(2):
                    v = data[i, :, pl.ds((q * 4 + a) * 256 + h * 128, 128)]
                    both.append(v * s[2 * a + h : 2 * a + h + 1, :])
                parts.append(jnp.concatenate(both, axis=1))
            block = jnp.concatenate(parts, axis=0)
            o = lax.dot_general(had_b[...], block, (((1,), (1,)), ((), ())), preferred_element_type=jnp.float32)
            g = (i * (64 // CHUNKS) + q) * (2 * STRIDE)
            first[pl.ds(g, 256), :] = o[:, :128]
            first[pl.ds(g + STRIDE, 256), :] = o[:, 128:]

    @pl.loop(0, 4)
    def _(i):
        for q in range(32):
            c = (i * 32 + q) * 2
            z0 = first[pl.ds(c, 128, stride=STRIDE), :].astype(jnp.bfloat16)
            z1 = first[pl.ds(c + 1, 128, stride=STRIDE), :].astype(jnp.bfloat16)
            o = jnp.dot(had_a[...], jnp.concatenate([z0, z1], axis=1), preferred_element_type=jnp.float32)
            second[pl.ds(pl.multiple_of(c * 128, 128), 128), :] = o[:, :128]
            second[pl.ds(pl.multiple_of(c * 128 + 128, 128), 128), :] = o[:, 128:]

    low = iota((128, 128), 1) < 64

    def gather(w, which):
        for u in range(2):
            for h in range(2):
                spot = (which * 2 + u) * 2 + h
                for b in range(8):
                    at = [rows_s[w, which * 4 + 2 * h + u, b * 16 + e] for e in range(16)]
                    got = [second[pl.ds(r, 1), :] for r in at]
                    for e in range(16):
                        picked[spot, pl.ds(b * 16 + e, 1), :] = got[e]

    def combine(which, j, dst, at_chip):
        for u in range(2):
            p = picked[(which * 2 + u) * 2]
            q = picked[(which * 2 + u) * 2 + 1]
            here = pl.ds(pl.multiple_of(j * 256 + u * 128, 128), 128)
            dst[at_chip, pl.ds(u * 128, 128), :] = (
                jnp.where(low, p, q) * sa[here, :] + pltpu.roll(jnp.where(low, q, p), 64, 1) * sb[here, :]
            )

    def to_pair(t):
        return pltpu.make_async_remote_copy(
            pair_out.at[t], pair_in.at[t], pair_send.at[t], pair_recv.at[t],
            device_id=(dp, 2 * chip + 1 - core), device_id_type=MESH,
        )

    def to_chip(t, slot):
        return pltpu.make_async_remote_copy(
            sum_out.at[t], sum_in.at[slot], sum_send.at[t], sum_recv.at[slot],
            device_id=(dp, 2 * t + core), device_id_type=MESH,
        )

    @pl.when(alone)
    def _():
        pl.semaphore_wait(barrier, 28)

    @pl.when(jnp.logical_not(alone))
    def _():
        pl.semaphore_wait(barrier, 29)

    def add_pair(t):
        to_pair(t).wait_recv()
        sum_out[t] = (own[t] + pair_in[t]).astype(jnp.bfloat16)
        to_chip(t, chip).start()

    window(0, 0).wait()
    gather(0, 0)

    @pl.loop(0, 4)
    def _(i):
        for w in range(2):
            t = served(i, w)
            gather(w, 1)
            combine(0, 2 * t + 1 - core, pair_out, t)
            to_pair(t).start()

            @pl.when(i < 3)
            def _():
                window(i + 1, w).start()

            if w == 0:
                window(i, 1).wait()
                gather(1, 0)
                combine(1, 2 * t + core, own, t)

                @pl.when(i > 0)
                def _():
                    add_pair(served(i - 1, 1))

            else:

                @pl.when(i < 3)
                def _():
                    window(i + 1, 0).wait()
                    gather(0, 0)
                    combine(1, 2 * t + core, own, t)
                    add_pair(served(i, 0))

                @pl.when(i == 3)
                def _():
                    add_pair(served(i, 0))
                    combine(1, 2 * t + core, own, t)

    to_pair(chip).wait_recv()
    total = own[chip] + pair_in[chip]
    for n in range(7):
        t = served(n // 2, n % 2)
        to_chip(t, t).wait_recv()
        total += sum_in[t].astype(jnp.float32)
    ring[z] = (total * SCALE).astype(jnp.bfloat16)

    def along(n, slot, part, sem):
        here = ring.at[slot, pl.ds(part * 128, 128)]
        return pltpu.make_async_remote_copy(
            here, here, ring_send.at[sem], ring_recv.at[slot, part],
            device_id=(2 * lax.rem(z + n, 8) + x, me), device_id_type=MESH,
        )

    sent = []

    def pass_on(n, slot, part):
        sent.append(along(n, slot, part, len(sent)))
        sent[-1].start()

    def arrived(slot, part):
        along(1, slot, part, 0).wait_recv()

    def at(n):
        return lax.rem(z + n, 8)

    to_x = pltpu.make_async_remote_copy(
        ring.at[z], beside, x_send, x_recv, device_id=(2 * z + 1 - x, me), device_id_type=MESH
    )
    for part in range(2):
        pass_on(2, z, part)
        pass_on(6, z, 1 - part)
    to_x.start()
    for part in range(2):
        pass_on(1, z, part)
        pass_on(7, z, part)

    def to_owner(k, d, m, slot):
        return pltpu.make_async_remote_copy(
            block_out.at[k], block_in.at[slot], block_send.at[k], block_recv.at[slot],
            device_id=(d, m), device_id_type=MESH,
        )

    def products(slot):
        p = jnp.dot(left_t[...], ring[slot], preferred_element_type=jnp.float32)
        low = iota((32, 128), 1) < 64
        for rel in range(2):
            lo, hi = p[rel * 128 : rel * 128 + 64], p[rel * 128 + 64 : rel * 128 + 128]
            a0, b0, a1, b1 = lo[:32], lo[32:], hi[:32], hi[32:]
            both = jnp.where(low, a0, b1) + pltpu.roll(jnp.where(low, b0, a1), 64, 1)
            if rel == 0:
                mine = jnp.logical_and(alone, slot == chip)

                @pl.when(mine)
                def _():
                    block_in[me] = both

                @pl.when(jnp.logical_not(mine))
                def _():
                    block_out[2 * slot] = both
                    to_owner(2 * slot, dp, 2 * slot + x, me).start()

            else:
                block_out[2 * slot + 1] = both
                to_owner(2 * slot + 1, 2 * z + 1 - x, 2 * slot + x, me).start()

    left_t[pl.ds(0, 128), :] = ring[z].astype(jnp.float32).T.astype(jnp.bfloat16)
    to_x.wait_recv()
    left_t[pl.ds(128, 128), :] = beside[...].astype(jnp.float32).T.astype(jnp.bfloat16)
    products(z)
    for n, part in ((6, 0), (2, 1)):
        arrived(at(n), part)
        pass_on(8 - n, at(n), part)
        pass_on(1 if n == 6 else 7, at(n), part)
    for n, part in ((6, 1), (2, 0)):
        arrived(at(n), part)
        pass_on(1 if n == 6 else 7, at(n), part)
    products(at(6))
    products(at(2))
    for n in (7, 1, 5, 3):
        arrived(at(n), 0)
        arrived(at(n), 1)
        products(at(n))
    along(2, at(4), 0, 0).wait_recv()
    along(6, at(4), 1, 0).wait_recv()
    products(at(4))

    @pl.loop(0, 16)
    def _(q):
        @pl.when(jnp.logical_not(jnp.logical_and(alone, q == me)))
        def _():
            to_owner(0, dp, me, q).wait_recv()

    result = block_in[0]
    for q in range(1, 16):
        result += block_in[q]
    out[pl.ds(0, 32), :] = result[:, :64]
    out[pl.ds(32, 32), :] = result[:, 64:]

    for t in range(8):
        to_pair(t).wait_send()
    for o in range(1, 8):
        to_chip(lax.rem(chip + o, 8), chip).wait_send()
    to_x.wait_send()
    for copy in sent:
        copy.wait_send()

    @pl.loop(0, 8)
    def _(slot):
        to_owner(2 * slot + 1, dp, me, me).wait_send()

        @pl.when(jnp.logical_not(jnp.logical_and(alone, slot == chip)))
        def _():
            to_owner(2 * slot, dp, me, me).wait_send()


def per_device(grads, sign_bits, columns):
    f32, bf16 = jnp.float32, jnp.bfloat16
    dma = pltpu.SemaphoreType.DMA
    return pl.pallas_call(
        kernel,
        out_shape=jax.ShapeDtypeStruct((ROWS, ROWS), f32),
        in_specs=[pl.BlockSpec(memory_space=pl.ANY)] * 3,
        out_specs=pl.BlockSpec(memory_space=pltpu.VMEM),
        scratch_shapes=[
            pltpu.VMEM((CHUNKS, ROWS, LOCAL // CHUNKS), bf16),
            pltpu.VMEM((512, 128), jnp.int32),
            pltpu.VMEM((64, 128), jnp.int32),
            pltpu.VMEM((8, 8, 128), jnp.int32),
            pltpu.SMEM((2, 8, 128), jnp.int32),
            pltpu.VMEM((128 * STRIDE, 128), f32),
            pltpu.VMEM((32768, 128), f32),
            pltpu.VMEM((8, 128, 128), f32),
            pltpu.VMEM((4096, 128), f32),
            pltpu.VMEM((4096, 128), f32),
            pltpu.VMEM((256, 256), bf16),
            pltpu.VMEM((128, 128), bf16),
            pltpu.VMEM((8, 256, 128), f32),
            pltpu.VMEM((8, 256, 128), f32),
            pltpu.VMEM((8, 256, 128), f32),
            pltpu.VMEM((8, 256, 128), bf16),
            pltpu.VMEM((8, 256, 128), bf16),
            pltpu.VMEM((8, 256, 128), bf16),
            pltpu.VMEM((256, 128), bf16),
            pltpu.VMEM((256, 256), bf16),
            pltpu.VMEM((16, 32, 128), f32),
            pltpu.VMEM((16, 32, 128), f32),
            dma((CHUNKS,)),
            dma((4,)),
            dma((8,)),
            dma((8,)),
            dma((8,)),
            dma((8,)),
            dma((14,)),
            dma((8, 2)),
            dma,
            dma,
            dma((16,)),
            dma((16,)),
        ],
        compiler_params=pltpu.CompilerParams(
            vmem_limit_bytes=60 * 2**20, collective_id=0, has_side_effects=True
        ),
    )(grads, sign_bits.reshape(512, 128), columns.reshape(64, 128))


def solution(mesh):
    return jax.shard_map(
        per_device,
        mesh=mesh,
        in_specs=(P("dp", "mp"), P("mp"), P()),
        out_specs=P("dp", "mp"),
        check_vma=False,
    )
```

```python
import functools

import jax
import jax.numpy as jnp
from jax import lax
from jax.experimental import pallas as pl
from jax.experimental.pallas import tpu as pltpu
from jax.sharding import PartitionSpec as P

SKETCH = 8192
ROWS = 64
LOCAL = 65536
CHUNKS = 2
STRIDE = 265
MESH = pl.DeviceIdType.MESH
SCALE = 1.0 / SKETCH**0.5


def parity(v, bits):
    p = v & 1
    for i in range(1, bits):
        p = p ^ ((v >> i) & 1)
    return p


def iota(shape, axis):
    return lax.broadcasted_iota(jnp.int32, shape, axis)


def hadamard(order, bits):
    both = iota((order, order), 0) & iota((order, order), 1)
    return (1 - 2 * parity(both, bits)).astype(jnp.float32).astype(jnp.bfloat16)


def kernel(
    grads, bits, columns, out,
    data, sign, cols, rows_v, rows_s, first, second, picked, sa, sb, had_b, had_a,
    pair_out, pair_in, own, sum_out, sum_in, ring, beside, left_t, block_out, block_in,
    gsem, ssem, pair_send, pair_recv, sum_send, sum_recv, ring_send, ring_recv, x_send, x_recv, block_send, block_recv,
):
    me = lax.axis_index("mp")
    dp = lax.axis_index("dp")
    core, chip = lax.rem(me, 2), me // 2
    x, z = lax.rem(dp, 2), dp // 2
    alone = x == core

    copy_sign = pltpu.make_async_copy(bits, sign, ssem.at[0])
    copy_cols = pltpu.make_async_copy(columns, cols, ssem.at[1])
    copy_cols.start()
    copy_sign.start()
    width = LOCAL // CHUNKS

    def chunk(i):
        return pltpu.make_async_copy(grads.at[:, pl.ds(i * width, width)], data.at[i], gsem.at[i])

    for i in range(CHUNKS):
        chunk(i).start()
    barrier = pltpu.get_barrier_semaphore()

    def greet(d, m):
        pl.semaphore_signal(barrier, inc=1, device_id=(d, m), device_id_type=MESH)

    greet(dp, 2 * chip + 1 - core)
    for o in range(1, 8):
        greet(dp, 2 * lax.rem(chip + o, 8) + core)
    greet(2 * z + 1 - x, me)
    for o in (1, 2, 6, 7):
        greet(2 * lax.rem(z + o, 8) + x, me)

    @pl.loop(0, 16)
    def _(q):
        @pl.when(jnp.logical_not(jnp.logical_and(alone, q == me)))
        def _():
            greet(2 * z + core, q)

    had_b[...] = hadamard(256, 8)
    had_a[...] = hadamard(128, 7)
    copy_cols.wait()
    cv = cols[...]
    at_rows = (((cv & 255) << 7) | ((cv & 65535) >> 9)).reshape(8, 8, 128)
    turned = pltpu.roll(at_rows, 4, 1)
    rows_v[0] = jnp.where(core == 1, at_rows, turned)
    rows_v[1] = jnp.where(core == 1, turned, at_rows)

    across, y = chip // 4, lax.rem(chip, 4)

    def served(i, w):
        dx = 1 - (i + 2 * w) // 3
        return 4 * lax.rem(across + dx, 2) + lax.rem(y + 2 - w + i, 4)

    def window(which, i, w):
        return pltpu.make_async_copy(
            rows_v.at[which, served(i, w)], rows_s.at[which, w], ssem.at[2 + 2 * which + w]
        )

    for which in range(2):
        for w in range(2):
            window(which, 0, w).start()
    eye = iota((128, 128), 0) == iota((128, 128), 1)
    halves = ((iota((256, 128), 0) >> 7) == (iota((256, 128), 1) >> 6)).astype(jnp.float32).astype(jnp.bfloat16)
    w = 1.0 - 2.0 * parity((cv >> 16) & me, 4).astype(jnp.float32)
    ws = w * (1.0 - 2.0 * ((cv >> 8) & 1).astype(jnp.float32))

    def spread(v1, v2):
        d = jnp.concatenate([jnp.where(eye, v1, 0.0), jnp.where(eye, v2, 0.0)], axis=1)
        return jnp.dot(d.astype(jnp.bfloat16), halves, preferred_element_type=jnp.float32)

    for j in range(16):
        for t in range(2):
            p, q = 4 * j + t, 4 * j + 2 + t
            sa[pl.ds(j * 256 + t * 128, 128), :] = spread(w[p : p + 1], ws[q : q + 1])
            sb[pl.ds(j * 256 + t * 128, 128), :] = spread(ws[p : p + 1], w[q : q + 1])
    copy_sign.wait()

    @pl.loop(0, CHUNKS)
    def _(i):
        chunk(i).wait()
        for q in range(64 // CHUNKS):
            s = (2 * sign[pl.ds(pl.multiple_of(i * (512 // CHUNKS) + q * 8, 8), 8), :] - 1).astype(jnp.float32).astype(jnp.bfloat16)
            parts = []
            for a in range(4):
                both = []
                for h in range(2):
                    v = data[i, :, pl.ds((q * 4 + a) * 256 + h * 128, 128)]
                    both.append(v * s[2 * a + h : 2 * a + h + 1, :])
                parts.append(jnp.concatenate(both, axis=1))
            block = jnp.concatenate(parts, axis=0)
            o = lax.dot_general(had_b[...], block, (((1,), (1,)), ((), ())), preferred_element_type=jnp.float32)
            g = (i * (64 // CHUNKS) + q) * (2 * STRIDE)
            first[pl.ds(g, 256), :] = o[:, :128]
            first[pl.ds(g + STRIDE, 256), :] = o[:, 128:]

    @pl.loop(0, 4)
    def _(i):
        for q in range(32):
            c = (i * 32 + q) * 2
            z0 = first[pl.ds(c, 128, stride=STRIDE), :].astype(jnp.bfloat16)
            z1 = first[pl.ds(c + 1, 128, stride=STRIDE), :].astype(jnp.bfloat16)
            o = jnp.dot(had_a[...], jnp.concatenate([z0, z1], axis=1), preferred_element_type=jnp.float32)
            second[pl.ds(pl.multiple_of(c * 128, 128), 128), :] = o[:, :128]
            second[pl.ds(pl.multiple_of(c * 128 + 128, 128), 128), :] = o[:, 128:]

    low = iota((128, 128), 1) < 64

    def gather(which, w):
        for u in range(2):
            for h in range(2):
                spot = (which * 2 + u) * 2 + h
                for b in range(8):
                    at = [rows_s[which, w, 2 * h + u, b * 16 + e] for e in range(16)]
                    got = [second[pl.ds(r, 1), :] for r in at]
                    for e in range(16):
                        picked[spot, pl.ds(b * 16 + e, 1), :] = got[e]

    def combine(which, j, dst, at_chip):
        for u in range(2):
            p = picked[(which * 2 + u) * 2]
            q = picked[(which * 2 + u) * 2 + 1]
            here = pl.ds(pl.multiple_of(j * 256 + u * 128, 128), 128)
            dst[at_chip, pl.ds(u * 128, 128), :] = (
                jnp.where(low, p, q) * sa[here, :] + pltpu.roll(jnp.where(low, q, p), 64, 1) * sb[here, :]
            )

    def to_pair(t):
        return pltpu.make_async_remote_copy(
            pair_out.at[t], pair_in.at[t], pair_send.at[t], pair_recv.at[t],
            device_id=(dp, 2 * chip + 1 - core), device_id_type=MESH,
        )

    def to_chip(t, slot):
        return pltpu.make_async_remote_copy(
            sum_out.at[t], sum_in.at[slot], sum_send.at[t], sum_recv.at[slot],
            device_id=(dp, 2 * t + core), device_id_type=MESH,
        )

    @pl.when(alone)
    def _():
        pl.semaphore_wait(barrier, 28)

    @pl.when(jnp.logical_not(alone))
    def _():
        pl.semaphore_wait(barrier, 29)

    def add_pair(t):
        to_pair(t).wait_recv()
        sum_out[t] = (own[t] + pair_in[t]).astype(jnp.bfloat16)
        to_chip(t, chip).start()

    def gather_next(i, w, refill):
        window(0, i, w).wait()
        gather(0, w)
        if refill is None:
            window(0, i + 1, w).start()
        else:

            @pl.when(refill)
            def _():
                window(0, i + 1, w).start()

    def send_pair(i, w):
        t = served(i, w)
        combine(0, 2 * t + 1 - core, pair_out, t)
        to_pair(t).start()

    gather_next(0, 0, None)
    send_pair(0, 0)
    gather_next(0, 1, None)

    @pl.loop(0, 4)
    def _(i):
        for w in range(2):
            t = served(i, w)
            window(1, i, w).wait()
            if w == 0:
                gather(1, 0)
                send_pair(i, 1)
            else:

                @pl.when(i < 3)
                def _():
                    gather(1, 1)
                    send_pair(i + 1, 0)

                @pl.when(i == 3)
                def _():
                    gather(1, 1)

            @pl.when(i < 3)
            def _():
                window(1, i + 1, w).start()
                gather_next(i + 1, w, i < 2)

            combine(1, 2 * t + core, own, t)
            if w == 0:
                add_pair(t)
            else:

                @pl.when(i < 3)
                def _():
                    add_pair(t)

    to_pair(chip).wait_recv()
    total = own[chip] + pair_in[chip]
    for n in range(7):
        t = served(n // 2, n % 2)
        to_chip(t, t).wait_recv()
        total += sum_in[t].astype(jnp.float32)
    ring[z] = (total * SCALE).astype(jnp.bfloat16)

    def along(n, slot, part, sem):
        here = ring.at[slot, pl.ds(part * 128, 128)]
        return pltpu.make_async_remote_copy(
            here, here, ring_send.at[sem], ring_recv.at[slot, part],
            device_id=(2 * lax.rem(z + n, 8) + x, me), device_id_type=MESH,
        )

    sent = []

    def pass_on(n, slot, part):
        sent.append(along(n, slot, part, len(sent)))
        sent[-1].start()

    def arrived(slot, part):
        along(1, slot, part, 0).wait_recv()

    def at(n):
        return lax.rem(z + n, 8)

    to_x = pltpu.make_async_remote_copy(
        ring.at[z], beside, x_send, x_recv, device_id=(2 * z + 1 - x, me), device_id_type=MESH
    )
    for part in range(2):
        pass_on(2, z, part)
        pass_on(6, z, 1 - part)
    to_x.start()
    for part in range(2):
        pass_on(1, z, part)
        pass_on(7, z, part)

    def to_owner(k, d, m, slot):
        return pltpu.make_async_remote_copy(
            block_out.at[k], block_in.at[slot], block_send.at[k], block_recv.at[slot],
            device_id=(d, m), device_id_type=MESH,
        )

    def products(slot):
        p = jnp.dot(left_t[...], ring[slot], preferred_element_type=jnp.float32)
        low = iota((32, 128), 1) < 64
        for rel in range(2):
            lo, hi = p[rel * 128 : rel * 128 + 64], p[rel * 128 + 64 : rel * 128 + 128]
            a0, b0, a1, b1 = lo[:32], lo[32:], hi[:32], hi[32:]
            both = jnp.where(low, a0, b1) + pltpu.roll(jnp.where(low, b0, a1), 64, 1)
            if rel == 0:
                mine = jnp.logical_and(alone, slot == chip)

                @pl.when(mine)
                def _():
                    block_in[me] = both

                @pl.when(jnp.logical_not(mine))
                def _():
                    block_out[2 * slot] = both
                    to_owner(2 * slot, dp, 2 * slot + x, me).start()

            else:
                block_out[2 * slot + 1] = both
                to_owner(2 * slot + 1, 2 * z + 1 - x, 2 * slot + x, me).start()

    left_t[pl.ds(0, 128), :] = ring[z].astype(jnp.float32).T.astype(jnp.bfloat16)
    to_x.wait_recv()
    left_t[pl.ds(128, 128), :] = beside[...].astype(jnp.float32).T.astype(jnp.bfloat16)
    products(z)
    late = lax.rem(z + 2, 8) // 4
    one, two, three = 1 + 6 * late, 2 + 4 * late, 3 + 2 * late

    def relay(n, back, part):
        for last in range(2):
            half = part + last - 2 * part * last
            arrived(at(n), half)
            if last == 0:
                pass_on(8 - n, at(n), half)
            pass_on(back, at(n), half)

    def take(n):
        arrived(at(n), 0)
        arrived(at(n), 1)
        products(at(n))

    relay(two, 8 - one, 1 - late)
    products(at(two))
    relay(8 - two, one, late)
    products(at(8 - two))
    take(one)
    take(8 - one)
    take(three)
    take(8 - three)
    along(2, at(4), 0, 0).wait_recv()
    along(6, at(4), 1, 0).wait_recv()
    products(at(4))

    @pl.loop(0, 16)
    def _(q):
        @pl.when(jnp.logical_not(jnp.logical_and(alone, q == me)))
        def _():
            to_owner(0, dp, me, q).wait_recv()

    result = block_in[0]
    for q in range(1, 16):
        result += block_in[q]
    out[pl.ds(0, 32), :] = result[:, :64]
    out[pl.ds(32, 32), :] = result[:, 64:]

    for t in range(8):
        to_pair(t).wait_send()
    for o in range(1, 8):
        to_chip(lax.rem(chip + o, 8), chip).wait_send()
    to_x.wait_send()
    for copy in sent:
        copy.wait_send()

    @pl.loop(0, 8)
    def _(slot):
        to_owner(2 * slot + 1, dp, me, me).wait_send()

        @pl.when(jnp.logical_not(jnp.logical_and(alone, slot == chip)))
        def _():
            to_owner(2 * slot, dp, me, me).wait_send()


def per_device(grads, sign_bits, columns):
    f32, bf16 = jnp.float32, jnp.bfloat16
    dma = pltpu.SemaphoreType.DMA
    return pl.pallas_call(
        kernel,
        out_shape=jax.ShapeDtypeStruct((ROWS, ROWS), f32),
        in_specs=[pl.BlockSpec(memory_space=pl.ANY)] * 3,
        out_specs=pl.BlockSpec(memory_space=pltpu.VMEM),
        scratch_shapes=[
            pltpu.VMEM((CHUNKS, ROWS, LOCAL // CHUNKS), bf16),
            pltpu.VMEM((512, 128), jnp.int32),
            pltpu.VMEM((64, 128), jnp.int32),
            pltpu.VMEM((2, 8, 8, 128), jnp.int32),
            pltpu.SMEM((2, 2, 8, 128), jnp.int32),
            pltpu.VMEM((128 * STRIDE, 128), f32),
            pltpu.VMEM((32768, 128), f32),
            pltpu.VMEM((8, 128, 128), f32),
            pltpu.VMEM((4096, 128), f32),
            pltpu.VMEM((4096, 128), f32),
            pltpu.VMEM((256, 256), bf16),
            pltpu.VMEM((128, 128), bf16),
            pltpu.VMEM((8, 256, 128), f32),
            pltpu.VMEM((8, 256, 128), f32),
            pltpu.VMEM((8, 256, 128), f32),
            pltpu.VMEM((8, 256, 128), bf16),
            pltpu.VMEM((8, 256, 128), bf16),
            pltpu.VMEM((8, 256, 128), bf16),
            pltpu.VMEM((256, 128), bf16),
            pltpu.VMEM((256, 256), bf16),
            pltpu.VMEM((16, 32, 128), f32),
            pltpu.VMEM((16, 32, 128), f32),
            dma((CHUNKS,)),
            dma((6,)),
            dma((8,)),
            dma((8,)),
            dma((8,)),
            dma((8,)),
            dma((14,)),
            dma((8, 2)),
            dma,
            dma,
            dma((16,)),
            dma((16,)),
        ],
        compiler_params=pltpu.CompilerParams(
            vmem_limit_bytes=60 * 2**20, collective_id=0, has_side_effects=True
        ),
    )(grads, sign_bits.reshape(512, 128), columns.reshape(64, 128))


def solution(mesh):
    return jax.shard_map(
        per_device,
        mesh=mesh,
        in_specs=(P("dp", "mp"), P("mp"), P()),
        out_specs=P("dp", "mp"),
        check_vma=False,
    )
```

```python
import functools

import jax
import jax.numpy as jnp
from jax import lax
from jax.experimental import pallas as pl
from jax.experimental.pallas import tpu as pltpu
from jax.sharding import PartitionSpec as P

SKETCH = 8192
ROWS = 64
LOCAL = 65536
CHUNKS = 2
STRIDE = 265
MESH = pl.DeviceIdType.MESH
SCALE = 1.0 / SKETCH**0.5


def parity(v, bits):
    p = v & 1
    for i in range(1, bits):
        p = p ^ ((v >> i) & 1)
    return p


def iota(shape, axis):
    return lax.broadcasted_iota(jnp.int32, shape, axis)


def hadamard(order, bits):
    both = iota((order, order), 0) & iota((order, order), 1)
    return (1 - 2 * parity(both, bits)).astype(jnp.float32).astype(jnp.bfloat16)


def kernel(
    grads, bits, columns, out,
    data, sign, cols, rows_v, rows_s, first, second, picked, sa, sb, had_b, had_a,
    pair_out, pair_in, own, sum_out, sum_in, ring, beside, left_t, block_out, block_in,
    gsem, ssem, pair_send, pair_recv, sum_send, sum_recv, ring_send, ring_recv, x_send, x_recv, block_send, block_recv,
):
    me = lax.axis_index("mp")
    dp = lax.axis_index("dp")
    core, chip = lax.rem(me, 2), me // 2
    x, z = lax.rem(dp, 2), dp // 2
    alone = x == core

    copy_sign = pltpu.make_async_copy(bits, sign, ssem.at[0])
    copy_cols = pltpu.make_async_copy(columns, cols, ssem.at[1])
    copy_cols.start()
    copy_sign.start()
    width = LOCAL // CHUNKS

    def chunk(i):
        return pltpu.make_async_copy(grads.at[:, pl.ds(i * width, width)], data.at[i], gsem.at[i])

    for i in range(CHUNKS):
        chunk(i).start()
    barrier = pltpu.get_barrier_semaphore()

    def greet(d, m):
        pl.semaphore_signal(barrier, inc=1, device_id=(d, m), device_id_type=MESH)

    greet(dp, 2 * chip + 1 - core)
    for o in range(1, 8):
        greet(dp, 2 * lax.rem(chip + o, 8) + core)
    greet(2 * z + 1 - x, me)
    for o in (1, 2, 6, 7):
        greet(2 * lax.rem(z + o, 8) + x, me)

    @pl.loop(0, 16)
    def _(q):
        @pl.when(jnp.logical_not(jnp.logical_and(alone, q == me)))
        def _():
            greet(2 * z + core, q)

    had_b[...] = hadamard(256, 8)
    had_a[...] = hadamard(128, 7)
    copy_cols.wait()
    cv = cols[...]
    at_rows = (((cv & 255) << 7) | ((cv & 65535) >> 9)).reshape(8, 8, 128)
    turned = pltpu.roll(at_rows, 4, 1)
    rows_v[0] = jnp.where(core == 1, at_rows, turned)
    rows_v[1] = jnp.where(core == 1, turned, at_rows)

    across, y = chip // 4, lax.rem(chip, 4)

    def served(i, w):
        dx = 1 - (i + 2 * w) // 3
        return 4 * lax.rem(across + dx, 2) + lax.rem(y + 2 - w + i, 4)

    def window(which, i, w):
        return pltpu.make_async_copy(
            rows_v.at[which, served(i, w)], rows_s.at[which, w], ssem.at[2 + 2 * which + w]
        )

    for which in range(2):
        for w in range(2):
            window(which, 0, w).start()
    eye = iota((128, 128), 0) == iota((128, 128), 1)
    halves = ((iota((256, 128), 0) >> 7) == (iota((256, 128), 1) >> 6)).astype(jnp.float32).astype(jnp.bfloat16)
    w = 1.0 - 2.0 * parity((cv >> 16) & me, 4).astype(jnp.float32)
    ws = w * (1.0 - 2.0 * ((cv >> 8) & 1).astype(jnp.float32))

    def spread(v1, v2):
        d = jnp.concatenate([jnp.where(eye, v1, 0.0), jnp.where(eye, v2, 0.0)], axis=1)
        return jnp.dot(d.astype(jnp.bfloat16), halves, preferred_element_type=jnp.float32)

    for j in range(16):
        for t in range(2):
            p, q = 4 * j + t, 4 * j + 2 + t
            sa[pl.ds(j * 256 + t * 128, 128), :] = spread(w[p : p + 1], ws[q : q + 1])
            sb[pl.ds(j * 256 + t * 128, 128), :] = spread(ws[p : p + 1], w[q : q + 1])
    copy_sign.wait()

    @pl.loop(0, CHUNKS)
    def _(i):
        chunk(i).wait()
        for q in range(64 // CHUNKS):
            s = (2 * sign[pl.ds(pl.multiple_of(i * (512 // CHUNKS) + q * 8, 8), 8), :] - 1).astype(jnp.float32).astype(jnp.bfloat16)
            parts = []
            for a in range(4):
                both = []
                for h in range(2):
                    v = data[i, :, pl.ds((q * 4 + a) * 256 + h * 128, 128)]
                    both.append(v * s[2 * a + h : 2 * a + h + 1, :])
                parts.append(jnp.concatenate(both, axis=1))
            block = jnp.concatenate(parts, axis=0)
            o = lax.dot_general(had_b[...], block, (((1,), (1,)), ((), ())), preferred_element_type=jnp.float32)
            g = (i * (64 // CHUNKS) + q) * (2 * STRIDE)
            first[pl.ds(g, 256), :] = o[:, :128]
            first[pl.ds(g + STRIDE, 256), :] = o[:, 128:]

    @pl.loop(0, 4)
    def _(i):
        for q in range(32):
            c = (i * 32 + q) * 2
            z0 = first[pl.ds(c, 128, stride=STRIDE), :].astype(jnp.bfloat16)
            z1 = first[pl.ds(c + 1, 128, stride=STRIDE), :].astype(jnp.bfloat16)
            o = jnp.dot(had_a[...], jnp.concatenate([z0, z1], axis=1), preferred_element_type=jnp.float32)
            second[pl.ds(pl.multiple_of(c * 128, 128), 128), :] = o[:, :128]
            second[pl.ds(pl.multiple_of(c * 128 + 128, 128), 128), :] = o[:, 128:]

    low = iota((128, 128), 1) < 64

    def gather(which, w):
        for u in range(2):
            for h in range(2):
                spot = (which * 2 + u) * 2 + h
                for b in range(8):
                    at = [rows_s[which, w, 2 * h + u, b * 16 + e] for e in range(16)]
                    got = [second[pl.ds(r, 1), :] for r in at]
                    for e in range(16):
                        picked[spot, pl.ds(b * 16 + e, 1), :] = got[e]

    def combine(which, j, dst, at_chip):
        for u in range(2):
            p = picked[(which * 2 + u) * 2]
            q = picked[(which * 2 + u) * 2 + 1]
            here = pl.ds(pl.multiple_of(j * 256 + u * 128, 128), 128)
            dst[at_chip, pl.ds(u * 128, 128), :] = (
                jnp.where(low, p, q) * sa[here, :] + pltpu.roll(jnp.where(low, q, p), 64, 1) * sb[here, :]
            )

    def to_pair(t):
        return pltpu.make_async_remote_copy(
            pair_out.at[t], pair_in.at[t], pair_send.at[t], pair_recv.at[t],
            device_id=(dp, 2 * chip + 1 - core), device_id_type=MESH,
        )

    def to_chip(t, slot):
        return pltpu.make_async_remote_copy(
            sum_out.at[t], sum_in.at[slot], sum_send.at[t], sum_recv.at[slot],
            device_id=(dp, 2 * t + core), device_id_type=MESH,
        )

    @pl.when(alone)
    def _():
        pl.semaphore_wait(barrier, 28)

    @pl.when(jnp.logical_not(alone))
    def _():
        pl.semaphore_wait(barrier, 29)

    def add_pair(t):
        to_pair(t).wait_recv()
        sum_out[t] = (own[t] + pair_in[t]).astype(jnp.bfloat16)
        to_chip(t, chip).start()

    def gather_next(i, w, refill):
        window(0, i, w).wait()
        gather(0, w)
        if refill is None:
            window(0, i + 1, w).start()
        else:

            @pl.when(refill)
            def _():
                window(0, i + 1, w).start()

    def send_pair(i, w):
        t = served(i, w)
        combine(0, 2 * t + 1 - core, pair_out, t)
        to_pair(t).start()

    gather_next(0, 0, None)
    send_pair(0, 0)
    gather_next(0, 1, None)

    @pl.loop(0, 4)
    def _(i):
        for w in range(2):
            t = served(i, w)
            window(1, i, w).wait()
            if w == 0:
                gather(1, 0)
                send_pair(i, 1)
            else:

                @pl.when(i < 3)
                def _():
                    gather(1, 1)
                    send_pair(i + 1, 0)

                @pl.when(i == 3)
                def _():
                    gather(1, 1)

            @pl.when(i < 3)
            def _():
                window(1, i + 1, w).start()
                gather_next(i + 1, w, i < 2)

            combine(1, 2 * t + core, own, t)
            if w == 0:
                add_pair(t)
            else:

                @pl.when(i < 3)
                def _():
                    add_pair(t)

    to_pair(chip).wait_recv()
    total = own[chip] + pair_in[chip]
    for n in range(7):
        t = served(n // 2, n % 2)
        to_chip(t, t).wait_recv()
        total += sum_in[t].astype(jnp.float32)
    ring[z] = (total * SCALE).astype(jnp.bfloat16)

    def along(n, slot, part, sem):
        here = ring.at[slot] if part is None else ring.at[slot, pl.ds(part * 128, 128)]
        return pltpu.make_async_remote_copy(
            here, here, ring_send.at[sem], ring_recv.at[slot, 0 if part is None else part],
            device_id=(2 * lax.rem(z + n, 8) + x, me), device_id_type=MESH,
        )

    sent = []

    def pass_on(n, slot, part):
        sent.append(along(n, slot, part, len(sent)))
        sent[-1].start()

    def arrived(slot, part):
        along(1, slot, part, 0).wait_recv()

    def at(n):
        return lax.rem(z + n, 8)

    to_x = pltpu.make_async_remote_copy(
        ring.at[z], beside, x_send, x_recv, device_id=(2 * z + 1 - x, me), device_id_type=MESH
    )
    for part in range(2):
        pass_on(2, z, part)
        pass_on(6, z, 1 - part)
    to_x.start()
    pass_on(1, z, None)
    pass_on(7, z, None)

    def to_owner(k, d, m, slot):
        return pltpu.make_async_remote_copy(
            block_out.at[k], block_in.at[slot], block_send.at[k], block_recv.at[slot],
            device_id=(d, m), device_id_type=MESH,
        )

    def products(slot):
        p = jnp.dot(left_t[...], ring[slot], preferred_element_type=jnp.float32)
        low = iota((32, 128), 1) < 64
        for rel in range(2):
            lo, hi = p[rel * 128 : rel * 128 + 64], p[rel * 128 + 64 : rel * 128 + 128]
            a0, b0, a1, b1 = lo[:32], lo[32:], hi[:32], hi[32:]
            both = jnp.where(low, a0, b1) + pltpu.roll(jnp.where(low, b0, a1), 64, 1)
            if rel == 0:
                mine = jnp.logical_and(alone, slot == chip)

                @pl.when(mine)
                def _():
                    block_in[me] = both

                @pl.when(jnp.logical_not(mine))
                def _():
                    block_out[2 * slot] = both
                    to_owner(2 * slot, dp, 2 * slot + x, me).start()

            else:
                block_out[2 * slot + 1] = both
                to_owner(2 * slot + 1, 2 * z + 1 - x, 2 * slot + x, me).start()

    left_t[pl.ds(0, 128), :] = ring[z].astype(jnp.float32).T.astype(jnp.bfloat16)
    to_x.wait_recv()
    left_t[pl.ds(128, 128), :] = beside[...].astype(jnp.float32).T.astype(jnp.bfloat16)
    products(z)
    late = lax.rem(z + 2, 8) // 4
    one, two, three = 1 + 6 * late, 2 + 4 * late, 3 + 2 * late

    def relay(n, back, part):
        for last in range(2):
            half = part + last - 2 * part * last
            arrived(at(n), half)
            if last == 0:
                pass_on(8 - n, at(n), half)
            pass_on(back, at(n), half)

    def take(n):
        arrived(at(n), 0)
        arrived(at(n), 1)
        products(at(n))

    relay(two, 8 - one, 1 - late)
    products(at(two))
    relay(8 - two, one, late)
    products(at(8 - two))
    for n in (one, 8 - one):
        arrived(at(n), None)
        products(at(n))
    take(three)
    take(8 - three)
    along(2, at(4), 0, 0).wait_recv()
    along(6, at(4), 1, 0).wait_recv()
    products(at(4))

    @pl.loop(0, 16)
    def _(q):
        @pl.when(jnp.logical_not(jnp.logical_and(alone, q == me)))
        def _():
            to_owner(0, dp, me, q).wait_recv()

    result = block_in[0]
    for q in range(1, 16):
        result += block_in[q]
    out[pl.ds(0, 32), :] = result[:, :64]
    out[pl.ds(32, 32), :] = result[:, 64:]

    for t in range(8):
        to_pair(t).wait_send()
    for o in range(1, 8):
        to_chip(lax.rem(chip + o, 8), chip).wait_send()
    to_x.wait_send()
    for copy in sent:
        copy.wait_send()

    @pl.loop(0, 8)
    def _(slot):
        to_owner(2 * slot + 1, dp, me, me).wait_send()

        @pl.when(jnp.logical_not(jnp.logical_and(alone, slot == chip)))
        def _():
            to_owner(2 * slot, dp, me, me).wait_send()


def per_device(grads, sign_bits, columns):
    f32, bf16 = jnp.float32, jnp.bfloat16
    dma = pltpu.SemaphoreType.DMA
    return pl.pallas_call(
        kernel,
        out_shape=jax.ShapeDtypeStruct((ROWS, ROWS), f32),
        in_specs=[pl.BlockSpec(memory_space=pl.ANY)] * 3,
        out_specs=pl.BlockSpec(memory_space=pltpu.VMEM),
        scratch_shapes=[
            pltpu.VMEM((CHUNKS, ROWS, LOCAL // CHUNKS), bf16),
            pltpu.VMEM((512, 128), jnp.int32),
            pltpu.VMEM((64, 128), jnp.int32),
            pltpu.VMEM((2, 8, 8, 128), jnp.int32),
            pltpu.SMEM((2, 2, 8, 128), jnp.int32),
            pltpu.VMEM((128 * STRIDE, 128), f32),
            pltpu.VMEM((32768, 128), f32),
            pltpu.VMEM((8, 128, 128), f32),
            pltpu.VMEM((4096, 128), f32),
            pltpu.VMEM((4096, 128), f32),
            pltpu.VMEM((256, 256), bf16),
            pltpu.VMEM((128, 128), bf16),
            pltpu.VMEM((8, 256, 128), f32),
            pltpu.VMEM((8, 256, 128), f32),
            pltpu.VMEM((8, 256, 128), f32),
            pltpu.VMEM((8, 256, 128), bf16),
            pltpu.VMEM((8, 256, 128), bf16),
            pltpu.VMEM((8, 256, 128), bf16),
            pltpu.VMEM((256, 128), bf16),
            pltpu.VMEM((256, 256), bf16),
            pltpu.VMEM((16, 32, 128), f32),
            pltpu.VMEM((16, 32, 128), f32),
            dma((CHUNKS,)),
            dma((6,)),
            dma((8,)),
            dma((8,)),
            dma((8,)),
            dma((8,)),
            dma((14,)),
            dma((8, 2)),
            dma,
            dma,
            dma((16,)),
            dma((16,)),
        ],
        compiler_params=pltpu.CompilerParams(
            vmem_limit_bytes=60 * 2**20, collective_id=0, has_side_effects=True
        ),
    )(grads, sign_bits.reshape(512, 128), columns.reshape(64, 128))


def solution(mesh):
    return jax.shard_map(
        per_device,
        mesh=mesh,
        in_specs=(P("dp", "mp"), P("mp"), P()),
        out_specs=P("dp", "mp"),
        check_vma=False,
    )
```
